256 devices in a mesh: row: 8 (over x, core), col: 32 (over z, y).
Axes of the slice: x: 4, y: 4, z: 8, core: 2. Of those that a mesh axis runs over, the one named last changes fastest.
Arguments:
- source_points: bfloat16 [16384, 256], P(('row', 'col')), may hold values from -96 to 96
- target_points: bfloat16 [65536, 256], P(('col', 'row')), may hold values from -6 to 6
- source_weight: float32 [16384], P('row'), may hold values from 0.25 to 4
- target_weight: float32 [65536], P('col'), may hold values from 0.25 to 4
- target_potential: float32 [65536], P('col'), may hold values from -8 to 104
Outputs:
- source_potential: float32 [16384], P('row')
- target_updated: float32 [65536], P('col')
The draws below stay inside these ranges and needn't reach their ends.
All inputs are finite; a program needn't handle non-finite values.
Results may differ from the reference program's by a relative error of at most 0.0003.
Values may be sent and summed in bfloat16 or wider, within the bound.
No kernel may reach another device: no remote copies, remote signals or barrier semaphores. Data moves between devices by JAX's collectives and lax.ppermute only.
A program may use at most 64 MiB of HBM per device.

```python
import math
import jax
import jax.numpy as jnp
from jax import lax

D = 256
NS = 16384
NT = 65536


def draw_source_points(key, part):
    key = jax.random.fold_in(key, 11)
    first_key = jax.random.fold_in(key, 0)
    values = jnp.clip(jax.random.normal(first_key, (NS, D), jnp.float32), -6.0, 6.0)
    return values.astype(jnp.bfloat16)


def draw_target_potential(key, part):
    key = jax.random.fold_in(key, 23)
    first_key = jax.random.fold_in(key, 0)
    values = jnp.clip(2.0 * jax.random.normal(first_key, (NT,), jnp.float32), -8.0, 8.0)
    return values


def level_of(rng, dims, cuts, smallest, largest):
    level, own = 1.0, jax.random.fold_in(rng, 6)
    for axis_at, shards_of in cuts:
        steps = jnp.exp(jax.random.uniform(jax.random.fold_in(own, axis_at), (shards_of,), jnp.float32, smallest / len(cuts), largest / len(cuts)))
        level = level * jnp.repeat(steps, dims[axis_at] // shards_of).reshape([-1 if axis == axis_at else 1 for axis in range(len(dims))])
    return level


def scatter_about(stream_key, shape, scale, bound, cuts=(), kind=jnp.bfloat16):
    gain = level_of(stream_key, shape, cuts, -0.22, 0.18) if cuts else 1.0
    drawn = jax.random.normal(stream_key, shape, jnp.float32) * scale * gain
    return jnp.minimum(jnp.maximum(drawn, -bound), bound).astype(kind)


def setup_inputs(seed: int = 0) -> dict:
    key_of = jax.random.split(jax.random.key(seed), 6)
    return {
        "source_points": draw_source_points(jax.random.fold_in(key_of[5], 71), 0),
        "target_points": scatter_about(key_of[1], (NT, D), 1.0, 6.0, ((0, 256),)),
        "source_weight": jnp.clip(jnp.exp(math.log(4.0) - 2.7725887 * jax.random.uniform(key_of[2], (NS,), jnp.float32) ** level_of(key_of[2], (NS,), ((0, 8),), -0.2, 0.2)), 0.25, 4.0),
        "target_weight": jnp.clip(jnp.exp(math.log(4.0) - 2.7725887 * jax.random.uniform(key_of[3], (NT,), jnp.float32) ** level_of(key_of[3], (NT,), ((0, 32),), -0.2, 0.2)), 0.25, 4.0),
        "target_potential": draw_target_potential(jax.random.fold_in(key_of[5], 71), 0),
    }


EPSILON = 0.25

def reference(source_points, target_points, source_weight, target_weight, target_potential):
    inverse_temp = 1.0 / (EPSILON * math.sqrt(D))
    source_rows = math.gcd(NS, 512)
    target_rows = math.gcd(NT, 512)

    def row_block(block):
        similar = jnp.dot(block, target_points.T, preferred_element_type=jnp.float32)
        logits = target_potential[None, :] + inverse_temp * similar
        highest = lax.optimization_barrier(jnp.max(logits, axis=1))
        return highest + jnp.log(lax.optimization_barrier(jnp.sum(jnp.exp(logits - highest[:, None]), axis=1)))
    row_lse = lax.map(row_block, source_points.reshape(NS // source_rows, source_rows, D)).reshape(NS)
    source_potential = jnp.log(source_weight) - (row_lse - jnp.float32(math.log(NT)))

    def col_block(block):
        similar = jnp.dot(source_points, block.T, preferred_element_type=jnp.float32)
        logits = source_potential[:, None] + inverse_temp * similar
        highest = lax.optimization_barrier(jnp.max(logits, axis=0))
        return highest + jnp.log(lax.optimization_barrier(jnp.sum(jnp.exp(logits - highest[None, :]), axis=0)))
    col_lse = lax.map(col_block, target_points.reshape(NT // target_rows, target_rows, D)).reshape(NT)
    target_updated = jnp.log(target_weight) - (col_lse - jnp.float32(math.log(NS)))
    return (source_potential, target_updated)
```

```python
import functools
import math

import jax
import jax.numpy as jnp
from jax import lax
from jax.experimental import pallas as pl
from jax.experimental.pallas import tpu as pltpu
from jax.sharding import Mesh
from jax.sharding import PartitionSpec as P

EPSILON = 0.25
LANES = 128
STRIP = 256
NX, NC, NZ, NY = 4, 2, 8, 4
SHIFTS = (0, 1, 3, 2)
VMEM = pl.BlockSpec(memory_space=pltpu.VMEM)
PARAMS = pltpu.CompilerParams(vmem_limit_bytes=40 * 1024 * 1024)


def contract(a, b):
    return lax.dot_general(a, b, (((1,), (1,)), ((), ())), preferred_element_type=jnp.float32)


def spread(row):
    return jnp.broadcast_to(row, (LANES, LANES)).T


def lse_of(buf, bias, rate):
    rows = buf.shape[0]
    step = 64
    out = []
    for half in range(STRIP // LANES):
        lanes = slice(half * LANES, (half + 1) * LANES)
        top = None
        for r in range(0, rows, step):
            value = buf[r : r + step, lanes] + bias[r : r + step, :]
            buf[r : r + step, lanes] = value
            top = value if top is None else jnp.maximum(top, value)
        top = jnp.max(top, axis=0, keepdims=True)
        total = None
        for r in range(0, rows, step):
            value = jnp.exp2((buf[r : r + step, lanes] - top) * rate)
            total = value if total is None else total + value
        total = jnp.sum(total, axis=0, keepdims=True)
        out.append(top + jnp.log2(total) / rate)
    return out


def all_strips(count, fill, finish, buf0, buf1):
    fill(0, buf0)

    def pair(p, _):
        fill(2 * p + 1, buf1)
        finish(2 * p, buf0)
        fill(jnp.minimum(2 * p + 2, count - 1), buf0)
        finish(2 * p + 1, buf1)
        return 0

    lax.fori_loop(0, count // 2, pair, 0)


def bias_kernel(tp_ref, bias_ref):
    x, c = lax.axis_index("x"), lax.axis_index("c")
    row = 0
    for other in range(NC):
        for k in SHIFTS:
            block = lax.rem(x - k + NX, NX) * NC + lax.rem(c + other, NC)
            for half in range(2):
                values = tp_ref[pl.ds(block * 2 + half, 1), :] * (1.0 / bias_kernel.scale)
                bias_ref[row * LANES : (row + 1) * LANES, :] = spread(values)
                row += 1


def row_kernel(rate, last, *refs):
    if last:
        s_ref, ta_ref, tb_ref, bias_ref, l0, l1, l2, out_ref, buf0, buf1, rows = refs
    else:
        s_ref, ta_ref, tb_ref, bias_ref, out_ref, buf0, buf1 = refs
    half = ta_ref.shape[0]
    got = []
    for n, buf in enumerate((buf0, buf1)):
        strip = s_ref[n * STRIP : (n + 1) * STRIP, :]
        buf[:half, :] = contract(ta_ref[...], strip)
        buf[half:, :] = contract(tb_ref[...], strip)
    for buf in (buf0, buf1):
        got += lse_of(buf, bias_ref, rate)
    mine = jnp.concatenate(got, axis=0)
    if not last:
        out_ref[...] = mine
        return
    y = lax.axis_index("y")
    for k, values in zip(SHIFTS, (l0[...], l1[...], l2[...], mine)):
        at = lax.rem(y - k + NY, NY) * 4
        for i in range(4):
            rows[pl.ds(at + i, 1), :] = values[i : i + 1, :]
    out_ref[...] = jnp.broadcast_to(rows[...][None], out_ref.shape)


def col_kernel(rate, scale, offset, got_ref, sw_ref, s0, s1, s2, s3, ta_ref, tb_ref, out_ref, sp_ref, buf0, buf1, bias, spu, cols):
    parts = got_ref[...]
    top = jnp.max(parts, axis=0)
    total = jnp.sum(jnp.exp2((parts - top[None]) * rate), axis=0)
    lse = top + jnp.log2(total) / rate
    sp = jnp.log(sw_ref[...]) - (lse * scale - offset)
    sp_ref[...] = sp
    spu[...] = sp * (1.0 / scale)
    x, c, y = lax.axis_index("x"), lax.axis_index("c"), lax.axis_index("y")
    row = 0
    for k in SHIFTS:
        at = lax.rem(y - k + NY, NY) * 4
        for i in range(4):
            bias[row * LANES : (row + 1) * LANES, :] = spread(spu[pl.ds(at + i, 1), :])
            row += 1
    chunk = s0.shape[0]
    for other, t_ref in enumerate((ta_ref, tb_ref)):
        core = lax.rem(c + other, NC)

        def fill(n, buf, t_ref=t_ref):
            strip = t_ref[pl.ds(pl.multiple_of(n * STRIP, STRIP), STRIP), :]
            for k, s_ref in enumerate((s0, s1, s2, s3)):
                buf[k * chunk : (k + 1) * chunk, :] = contract(s_ref[...], strip)

        def finish(n, buf, core=core):
            lo, hi = lse_of(buf, bias, rate)
            k = jnp.where(n == 2, 3, jnp.where(n == 3, 2, n))
            block = lax.rem(x - k + NX, NX) * NC + core
            cols[pl.ds(block * 2, 1), :] = lo
            cols[pl.ds(block * 2 + 1, 1), :] = hi

        all_strips(NX, fill, finish, buf0, buf1)
    out_ref[...] = jnp.broadcast_to(cols[...][None], out_ref.shape)


def last_kernel(rate, scale, offset, got_ref, tw_ref, out_ref):
    parts = got_ref[...]
    top = jnp.max(parts, axis=0)
    total = jnp.sum(jnp.exp2((parts - top[None]) * rate), axis=0)
    lse = top + jnp.log2(total) / rate
    out_ref[...] = jnp.log(tw_ref[...]) - (lse * scale - offset)


def cost(pairs, width):
    return pl.CostEstimate(flops=2 * pairs * width, bytes_accessed=8 * 1024 * 1024, transcendentals=pairs)


def per_device(source_points, target_points, source_weight, target_weight, target_potential):
    width = source_points.shape[1]
    scale = 1.0 / (EPSILON * math.sqrt(width))
    rate = scale * math.log2(math.e)
    n_rows, n_cols = source_weight.shape[0], target_weight.shape[0]
    f32 = jnp.float32
    sub = n_rows // LANES

    around = lambda n, k: [(i, (i + k) % n) for i in range(n)]
    pieces = [target_points] + [lax.ppermute(target_points, "x", around(NX, k)) for k in SHIFTS[1:]]
    near = jnp.concatenate(pieces, axis=0)
    far = lax.ppermute(near, "c", around(NC, 1))
    own = lax.all_to_all(jnp.broadcast_to(source_points[None], (NZ,) + source_points.shape), "z", 0, 0)
    own = own.reshape(-1, width)
    chunks = [own] + [lax.ppermute(own, "y", around(NY, k)) for k in SHIFTS[1:]]
    chunk = own.shape[0]

    bias_kernel.scale = scale
    bias = pl.pallas_call(
        bias_kernel,
        out_shape=jax.ShapeDtypeStruct((n_cols, LANES), f32),
        in_specs=[VMEM],
        out_specs=VMEM,
        compiler_params=PARAMS,
    )(target_potential.reshape(-1, LANES))

    bufs = [pltpu.VMEM((n_cols, STRIP), f32)] * 2
    lses = []
    for n in range(3):
        lses.append(
            pl.pallas_call(
                functools.partial(row_kernel, rate, False),
                out_shape=jax.ShapeDtypeStruct((chunk // LANES, LANES), f32),
                in_specs=[VMEM] * 4,
                out_specs=VMEM,
                scratch_shapes=bufs,
                compiler_params=PARAMS,
                cost_estimate=cost(chunk * n_cols, width),
            )(chunks[n], near, far, bias)
        )
    sent = pl.pallas_call(
        functools.partial(row_kernel, rate, True),
        out_shape=jax.ShapeDtypeStruct((NZ * NY, sub, LANES), f32),
        in_specs=[VMEM] * 7,
        out_specs=VMEM,
        scratch_shapes=bufs + [pltpu.VMEM((sub, LANES), f32)],
        compiler_params=PARAMS,
        cost_estimate=cost(chunk * n_cols, width),
    )(chunks[3], near, far, bias, *lses)
    got = lax.all_to_all(sent, ("z", "y"), 0, 0)

    small = n_rows // (NZ * NY)
    weight = source_weight.reshape(NZ, NY, small).transpose(1, 0, 2).reshape(sub, LANES)
    sent, potential = pl.pallas_call(
        functools.partial(col_kernel, rate, scale, math.log(n_cols * NZ * NY)),
        out_shape=[
            jax.ShapeDtypeStruct((NX * NC, n_cols // LANES, LANES), f32),
            jax.ShapeDtypeStruct((sub, LANES), f32),
        ],
        in_specs=[VMEM] * 8,
        out_specs=[VMEM] * 2,
        scratch_shapes=bufs
        + [pltpu.VMEM((n_rows, LANES), f32), pltpu.VMEM((sub, LANES), f32), pltpu.VMEM((n_cols // LANES, LANES), f32)],
        compiler_params=PARAMS,
        cost_estimate=cost(n_rows * n_cols, width),
    )(got, weight, *chunks, near, far)
    got = lax.all_to_all(sent, ("x", "c"), 0, 0)
    updated = pl.pallas_call(
        functools.partial(last_kernel, rate, scale, math.log(n_rows * NX * NC)),
        out_shape=jax.ShapeDtypeStruct((n_cols // LANES, LANES), f32),
        in_specs=[VMEM] * 2,
        out_specs=VMEM,
        compiler_params=PARAMS,
    )(got, target_weight.reshape(-1, LANES))
    potential = potential.reshape(NY, NZ, small).transpose(1, 0, 2).reshape(-1)
    return potential, updated.reshape(-1)


def solution(mesh):
    grid = Mesh(mesh.devices.reshape(NX, NC, NZ, NY), ("x", "c", "z", "y"))
    return jax.shard_map(
        per_device,
        mesh=grid,
        in_specs=(P(("x", "c", "z", "y"), None), P(("z", "y", "x", "c"), None), P(("x", "c")), P(("z", "y")), P(("z", "y"))),
        out_specs=(P(("x", "c")), P(("z", "y"))),
        check_vma=False,
    )
```

```python
import functools
import math

import jax
import jax.numpy as jnp
from jax import lax
from jax.experimental import pallas as pl
from jax.experimental.pallas import tpu as pltpu
from jax.sharding import Mesh
from jax.sharding import PartitionSpec as P

EPSILON = 0.25
LANES = 128
STRIP = 256
STEP = 64
NX, NC, NZ, NY = 4, 2, 8, 4
SHIFTS = (0, 1, 3, 2)
SAFE = 2.0**-90
VMEM = pl.BlockSpec(memory_space=pltpu.VMEM)
MIB = 1024 * 1024
f32 = jnp.float32


def params(mib):
    return pltpu.CompilerParams(vmem_limit_bytes=mib * MIB)


def contract(a, b):
    return lax.dot_general(a, b, (((1,), (1,)), ((), ())), preferred_element_type=f32)


def spread(row):
    return jnp.broadcast_to(row, (LANES, LANES)).T


def spread_rows(rows_of, count, out):
    for n in range(count):
        out[n * LANES : (n + 1) * LANES, :] = spread(rows_of(n))


def halves():
    return [(h, slice(h * LANES, (h + 1) * LANES)) for h in range(STRIP // LANES)]


def add_and_top(buf, bias, base, lanes):
    top = None
    for r in range(0, buf.shape[0], STEP):
        value = buf[r : r + STEP, lanes] + bias[base + r : base + r + STEP, :]
        buf[r : r + STEP, lanes] = value
        top = value if top is None else jnp.maximum(top, value)
    return jnp.max(top, axis=0, keepdims=True)


def sum_exp(buf, top, lanes, rate):
    total = None
    for r in range(0, buf.shape[0], STEP):
        value = jnp.exp2((buf[r : r + STEP, lanes] - top) * rate)
        total = value if total is None else total + value
    return jnp.sum(total, axis=0, keepdims=True)


def lse_of(buf, bias, rate, base=0):
    out = []
    for _, lanes in halves():
        top = add_and_top(buf, bias, base, lanes)
        out.append(top + jnp.log2(sum_exp(buf, top, lanes, rate)) / rate)
    return out


def lse_parts(parts, rate):
    top = jnp.max(parts, axis=0)
    total = jnp.sum(jnp.exp2((parts - top[None]) * rate), axis=0)
    return top + jnp.log2(total) / rate


def all_strips(count, fill, finish, buf0, buf1):
    fill(0, buf0)

    def pair(p, _):
        fill(2 * p + 1, buf1)
        finish(2 * p, buf0)
        fill(jnp.minimum(2 * p + 2, count - 2), buf0)
        finish(2 * p + 1, buf1)
        return 0

    lax.fori_loop(0, count // 2, pair, 0)


def shift_of(n):
    return jnp.where(n == 2, 3, jnp.where(n == 3, 2, n))


def join_kernel(scale, own_ref, pair_ref, gate_ref, *refs):
    del gate_ref
    *pieces, near_ref, bias_ref = refs
    at = 0
    for piece in pieces:
        near_ref[at : at + piece.shape[0], :] = piece[...]
        at += piece.shape[0]
    x, c = lax.axis_index("x"), lax.axis_index("c")
    row = 0
    for other in range(NC):
        for ref in (own_ref, pair_ref):
            for k in SHIFTS:
                block = lax.rem(x - k + NX, NX) * NC + lax.rem(c + other, NC)
                for half in range(2):
                    values = ref[pl.ds(block * 2 + half, 1), :] * (1.0 / scale)
                    bias_ref[row * LANES : (row + 1) * LANES, :] = spread(values)
                    row += 1


def products(s_ref, t_ref, bufs):
    for n, buf in enumerate(bufs):
        buf[...] = contract(t_ref[...], s_ref[n * STRIP : (n + 1) * STRIP, :])


def row_first(rate, s_ref, t_ref, bias_ref, out_ref, buf0, buf1):
    products(s_ref, t_ref, (buf0, buf1))
    out_ref[...] = jnp.concatenate(lse_of(buf0, bias_ref, rate) + lse_of(buf1, bias_ref, rate), axis=0)


def row_second(rate, s_ref, t_ref, bias_ref, first_ref, out_ref, buf0, buf1):
    products(s_ref, t_ref, (buf0, buf1))
    base = t_ref.shape[0]
    mine = jnp.concatenate(lse_of(buf0, bias_ref, rate, base) + lse_of(buf1, bias_ref, rate, base), axis=0)
    out_ref[...] = lse_parts(jnp.stack([first_ref[...], mine]), rate)


def row_third(rate, s_ref, ta_ref, tb_ref, bias_ref, own_ref, out_ref, rows_ref, buf0, buf1, buf2, buf3):
    products(s_ref, ta_ref, (buf0, buf1))
    products(s_ref, tb_ref, (buf2, buf3))
    base = ta_ref.shape[0]
    near = jnp.concatenate(lse_of(buf0, bias_ref, rate) + lse_of(buf1, bias_ref, rate), axis=0)
    far = jnp.concatenate(lse_of(buf2, bias_ref, rate, base) + lse_of(buf3, bias_ref, rate, base), axis=0)
    pair = lse_parts(jnp.stack([near, far]), rate)
    own = own_ref[...]
    low = lax.rem(lax.axis_index("y"), 2) == 0
    rows = jnp.concatenate([jnp.where(low, own, pair), jnp.where(low, pair, own)], axis=0)
    rows_ref[...] = rows
    out_ref[...] = jnp.broadcast_to(rows[None], out_ref.shape)


def row_order(scratch):
    half = scratch.shape[0] // 2
    own = lax.rem(lax.axis_index("y"), 2)

    def row(n):
        at = jnp.where(own == n // half, 0, half)
        return scratch[pl.ds(at + n % half, 1), :]

    return row


def fill_strip(t_ref, sources):
    def fill(n, buf):
        strip = t_ref[pl.ds(pl.multiple_of(n * STRIP, STRIP), STRIP), :]
        at = 0
        for s_ref in sources:
            buf[at : at + s_ref.shape[0], :] = contract(s_ref[...], strip)
            at += s_ref.shape[0]

    return fill


def swap_halves(even, odd):
    low = lax.broadcasted_iota(jnp.int32, even.shape, 1) < LANES // 2
    turn = functools.partial(pltpu.roll, shift=LANES // 2, axis=1)
    return jnp.where(low, even, turn(odd)), jnp.where(low, turn(even), odd)


def fold(value, op):
    out = value[:STEP]
    for r in range(STEP, value.shape[0], STEP):
        out = op(out, value[r : r + STEP])
    return out


def over_strip(sources, bias, strip, each, op):
    got = [None] * (STRIP // LANES)
    at = 0
    for s_ref in sources:
        for r in range(0, s_ref.shape[0], STRIP):
            product = contract(s_ref[r : r + STRIP, :], strip)
            for h, lanes in halves():
                value = fold(each(h, product[:, lanes] + bias[at : at + STRIP, :]), op)
                got[h] = value if got[h] is None else op(got[h], value)
            at += STRIP
    return got


def strips_of(*targets):
    strip = 0
    for t_ref in targets:
        for r in range(0, t_ref.shape[0], STRIP):
            yield strip, t_ref[r : r + STRIP, :]
            strip += 1


def early_kernel(rate, scale, offset, rows_ref, sw_ref, s0, s1, ta_ref, tb_ref, top_ref, ready_ref, bias, ahead):
    high = lax.axis_index("y") // 2
    rows = [sw_ref[pl.ds(2 * z + high, 1), :] for z in range(NZ)]
    weight = jnp.concatenate(swap_halves(jnp.concatenate(rows[0::2], axis=0), jnp.concatenate(rows[1::2], axis=0)), axis=0)
    ready = (jnp.log(weight) + offset) * (1.0 / scale)
    ready_ref[...] = ready
    ahead[...] = ready - rows_ref[...]
    spread_rows(row_order(ahead), bias.shape[0] // LANES, bias)
    for n, strip in strips_of(ta_ref, tb_ref):
        tops = over_strip((s0, s1), bias, strip, lambda h, value: value, jnp.maximum)
        for h, top in enumerate(tops):
            top_ref[2 * n + h : 2 * n + h + 1, :] = jnp.max(top, axis=0, keepdims=True)


def col_kernel(rate, got_ref, rows_ref, ready_ref, top_ref, s0, s1, ta_ref, tb_ref, out_ref, buf0, buf1, bias, ahead, cols, worst):
    lse = lse_parts(got_ref[...], rate)
    potential = ready_ref[...] - lse
    least = jnp.min(lse - rows_ref[...])
    ahead[...] = potential
    spread_rows(row_order(ahead), bias.shape[0] // LANES, bias)
    count = ta_ref.shape[0] // STRIP
    x, c, y = lax.axis_index("x"), lax.axis_index("c"), lax.axis_index("y")
    mine = jnp.where(y >= 2, 1, 0)

    def put(strip, values):
        core = lax.rem(c + strip // count, NC)
        at = lax.rem(strip, count)
        block = lax.rem(x - shift_of(lax.rem(at, NX)) + NX, NX) * NC + core
        side = jnp.where(at < NX, mine, 1 - mine)
        for h, value in enumerate(values):
            cols[side, pl.ds(block * 2 + h, 1), :] = value

    low = None
    for n, strip in strips_of(ta_ref, tb_ref):
        tops = [top_ref[2 * n + h : 2 * n + h + 1, :] - least for h in range(STRIP // LANES)]
        parts = over_strip((s0, s1), bias, strip, lambda h, value: jnp.exp2((value - tops[h]) * rate), jnp.add)
        totals = [jnp.sum(part, axis=0, keepdims=True) for part in parts]
        for total in totals:
            low = total if low is None else jnp.minimum(low, total)
        put(jnp.int32(n), [top + jnp.log2(total) / rate for top, total in zip(tops, totals)])
    worst[...] = low

    @pl.when(jnp.logical_not(jnp.min(worst[...]) >= SAFE))
    def _():
        for other, t_ref in enumerate((ta_ref, tb_ref)):

            def finish(n, buf, other=other):
                put(other * count + n, lse_of(buf, bias, rate))

            all_strips(count, fill_strip(t_ref, (s0, s1)), finish, buf0, buf1)

    for n in range(out_ref.shape[0]):
        out_ref[n, : cols.shape[1], :] = cols[n % 2]
        out_ref[n, cols.shape[1] :, :] = potential


def last_kernel(rate, scale, offset, got_ref, tw_ref, sp_ref, out_ref):
    n_cols = tw_ref.shape[0]
    out_ref[...] = jnp.log(tw_ref[...]) - (lse_parts(got_ref[:, :n_cols, :], rate) * scale - offset)
    place = 2 * (lax.axis_index("x") * NC + lax.axis_index("c"))
    for n in range(2):
        rows = got_ref[place + n, n_cols:, :] * scale
        half = rows.shape[0] // 2
        for odd, part in enumerate(swap_halves(rows[:half], rows[half:])):
            for j in range(half):
                at = 4 * j + 2 * odd + n
                sp_ref[at : at + 1, :] = part[j : j + 1, :]


def cost(mib, flops=0):
    return pl.CostEstimate(flops=int(flops), bytes_accessed=int(mib * MIB), transcendentals=0)


def per_device(source_points, target_points, source_weight, target_weight, target_potential):
    width = source_points.shape[1]
    scale = 1.0 / (EPSILON * math.sqrt(width))
    rate = scale * math.log2(math.e)
    n_rows, n_cols = source_weight.shape[0], target_weight.shape[0]
    rows_all, cols_all = n_rows * NX * NC, n_cols * NZ * NY
    half_rows = n_rows // 2

    def around(n, k):
        return [(i, (i + k) % n) for i in range(n)]

    beside = [(i, i ^ 1) for i in range(NY)]
    across = [(i, i ^ 3) for i in range(NY)]
    z_beside = [[z * NY + y for z in range(NZ) for y in p] for p in ((0, 1), (2, 3))]
    xc_across = [[n * NY + y for n in range(NX * NC) for y in p] for p in ((0, 3), (1, 2))]

    potential = target_potential.reshape(-1, LANES)
    copies = jnp.broadcast_to(source_points[None], (NZ,) + source_points.shape)
    pair_points = lax.ppermute(target_points, "y", across)
    pair_potential = lax.ppermute(potential, "y", across)
    pieces = [lax.ppermute(points, "x", around(NX, k)) if k else points for points in (target_points, pair_points) for k in SHIFTS]
    own = lax.all_to_all(copies, "z", 0, 0).reshape(-1, width)
    block = len(pieces) * target_points.shape[0]
    near, bias = pl.pallas_call(
        functools.partial(join_kernel, scale),
        out_shape=[jax.ShapeDtypeStruct((block, width), jnp.bfloat16), jax.ShapeDtypeStruct((2 * block, LANES), f32)],
        in_specs=[VMEM, VMEM, pl.BlockSpec(memory_space=pl.ANY)] + [VMEM] * len(pieces),
        out_specs=[VMEM] * 2,
        compiler_params=params(16),
        cost_estimate=cost(8),
    )(potential, pair_potential, own, *pieces)
    far = lax.ppermute(near, "c", around(NC, 1))
    pair = lax.ppermute(own, "y", beside)
    chunk = own.shape[0]
    sub = half_rows // LANES

    buf = pltpu.VMEM((block, STRIP), f32)
    part = jax.ShapeDtypeStruct((chunk // LANES, LANES), f32)
    first = pl.pallas_call(
        functools.partial(row_first, rate),
        out_shape=part,
        in_specs=[VMEM] * 3,
        out_specs=VMEM,
        scratch_shapes=[buf] * 2,
        compiler_params=params(16),
        cost_estimate=cost(1, 4e10),
    )(own, near, bias)
    second = pl.pallas_call(
        functools.partial(row_second, rate),
        out_shape=part,
        in_specs=[VMEM] * 4,
        out_specs=VMEM,
        scratch_shapes=[buf] * 2,
        compiler_params=params(16),
        cost_estimate=cost(0.25),
    )(own, far, bias, first)
    sent, rows = pl.pallas_call(
        functools.partial(row_third, rate),
        out_shape=[jax.ShapeDtypeStruct((2 * NZ, sub, LANES), f32), jax.ShapeDtypeStruct((sub, LANES), f32)],
        in_specs=[VMEM] * 5,
        out_specs=[VMEM] * 2,
        scratch_shapes=[buf] * 4,
        compiler_params=params(16),
        cost_estimate=cost(16),
    )(pair, near, far, bias, second)
    got = lax.all_to_all(sent, ("z", "y"), 0, 0, axis_index_groups=z_beside)

    strips = 2 * block // STRIP
    held = [pltpu.VMEM((half_rows, LANES), f32), pltpu.VMEM((sub, LANES), f32)]
    tops, ready = pl.pallas_call(
        functools.partial(early_kernel, rate, scale, math.log(cols_all)),
        out_shape=[jax.ShapeDtypeStruct((2 * strips, LANES), f32), jax.ShapeDtypeStruct((sub, LANES), f32)],
        in_specs=[VMEM] * 6,
        out_specs=[VMEM] * 2,
        scratch_shapes=held,
        compiler_params=params(16),
        cost_estimate=cost(16),
    )(rows, source_weight.reshape(-1, LANES), own, pair, near, far)
    sent = pl.pallas_call(
        functools.partial(col_kernel, rate),
        out_shape=jax.ShapeDtypeStruct((2 * NX * NC, n_cols // LANES + sub, LANES), f32),
        in_specs=[VMEM] * 8,
        out_specs=VMEM,
        scratch_shapes=[pltpu.VMEM((half_rows, STRIP), f32)] * 2 + held + [pltpu.VMEM((2, n_cols // LANES, LANES), f32), pltpu.VMEM((1, LANES), f32)],
        compiler_params=params(16),
        cost_estimate=cost(16),
    )(got, rows, ready, tops, own, pair, near, far)
    got = lax.all_to_all(sent, ("x", "c", "y"), 0, 0, axis_index_groups=xc_across)
    potential, updated = pl.pallas_call(
        functools.partial(last_kernel, rate, scale, math.log(rows_all)),
        out_shape=[jax.ShapeDtypeStruct((n // LANES, LANES), f32) for n in (n_rows, n_cols)],
        in_specs=[VMEM] * 2,
        out_specs=[VMEM] * 2,
        compiler_params=params(16),
    )(got, target_weight.reshape(-1, LANES))
    return potential.reshape(-1), updated.reshape(-1)


def solution(mesh):
    grid = Mesh(mesh.devices.reshape(NX, NC, NZ, NY), ("x", "c", "z", "y"))
    return jax.shard_map(
        per_device,
        mesh=grid,
        in_specs=(P(("x", "c", "z", "y"), None), P(("z", "y", "x", "c"), None), P(("x", "c")), P(("z", "y")), P(("z", "y"))),
        out_specs=(P(("x", "c")), P(("z", "y"))),
        check_vma=False,
    )
```

```python
import functools
import math

import jax
import jax.numpy as jnp
from jax import lax
from jax.experimental import pallas as pl
from jax.experimental.pallas import tpu as pltpu
from jax.sharding import Mesh
from jax.sharding import PartitionSpec as P

EPSILON = 0.25
LANES = 128
STRIP = 256
STEP = 64
NX, NC, NZ, NY = 4, 2, 8, 4
SHIFTS = (0, 1, 3, 2)
SAFE = 2.0**-90
VMEM = pl.BlockSpec(memory_space=pltpu.VMEM)
MIB = 1024 * 1024
f32 = jnp.float32


def params(mib):
    return pltpu.CompilerParams(vmem_limit_bytes=mib * MIB)


def contract(a, b):
    return lax.dot_general(a, b, (((1,), (1,)), ((), ())), preferred_element_type=f32)


def spread(row):
    return jnp.broadcast_to(row, (LANES, LANES)).T


def spread_rows(rows_of, count, out):
    for n in range(count):
        out[n * LANES : (n + 1) * LANES, :] = spread(rows_of(n))


def halves():
    return [(h, slice(h * LANES, (h + 1) * LANES)) for h in range(STRIP // LANES)]


def add_and_top(buf, bias, base, lanes):
    top = None
    for r in range(0, buf.shape[0], STEP):
        value = buf[r : r + STEP, lanes] + bias[base + r : base + r + STEP, :]
        buf[r : r + STEP, lanes] = value
        top = value if top is None else jnp.maximum(top, value)
    return jnp.max(top, axis=0, keepdims=True)


def sum_exp(buf, top, lanes, rate):
    total = None
    for r in range(0, buf.shape[0], STEP):
        value = jnp.exp2((buf[r : r + STEP, lanes] - top) * rate)
        total = value if total is None else total + value
    return jnp.sum(total, axis=0, keepdims=True)


def lse_of(buf, bias, rate, base=0):
    out = []
    for _, lanes in halves():
        top = add_and_top(buf, bias, base, lanes)
        out.append(top + jnp.log2(sum_exp(buf, top, lanes, rate)) / rate)
    return out


def lse_parts(parts, rate):
    top = jnp.max(parts, axis=0)
    total = jnp.sum(jnp.exp2((parts - top[None]) * rate), axis=0)
    return top + jnp.log2(total) / rate


def all_strips(count, fill, finish, buf0, buf1):
    fill(0, buf0)

    def pair(p, _):
        fill(2 * p + 1, buf1)
        finish(2 * p, buf0)
        fill(jnp.minimum(2 * p + 2, count - 2), buf0)
        finish(2 * p + 1, buf1)
        return 0

    lax.fori_loop(0, count // 2, pair, 0)


def shift_of(n):
    return jnp.where(n == 2, 3, jnp.where(n == 3, 2, n))


def join_kernel(scale, gate_ref, own_ref, pair_ref, *refs):
    del gate_ref
    *pieces, near_ref, bias_ref = refs
    at = 0
    for piece in pieces:
        near_ref[at : at + piece.shape[0], :] = piece[...]
        at += piece.shape[0]
    x, c = lax.axis_index("x"), lax.axis_index("c")

    def put(ref, side):
        row = 0
        for other in range(NC):
            for k in SHIFTS:
                block = lax.rem(x - k + NX, NX) * NC + lax.rem(c + other, NC)
                for half in range(2):
                    values = ref[pl.ds(block * 2 + half, 1), :] * (1.0 / scale)
                    at = (row + 2 * side + half) * LANES
                    bias_ref[at : at + LANES, :] = spread(values)
                row += 4

    put(own_ref, 0)
    put(pair_ref, 1)


def products(s_ref, t_ref, bufs):
    for n, buf in enumerate(bufs):
        buf[...] = contract(t_ref[...], s_ref[n * STRIP : (n + 1) * STRIP, :])


def row_first(rate, s_ref, t_ref, bias_ref, out_ref, buf0, buf1):
    products(s_ref, t_ref, (buf0, buf1))
    out_ref[...] = jnp.concatenate(lse_of(buf0, bias_ref, rate) + lse_of(buf1, bias_ref, rate), axis=0)


def row_second(rate, s_ref, t_ref, bias_ref, first_ref, out_ref, buf0, buf1):
    products(s_ref, t_ref, (buf0, buf1))
    base = t_ref.shape[0]
    mine = jnp.concatenate(lse_of(buf0, bias_ref, rate, base) + lse_of(buf1, bias_ref, rate, base), axis=0)
    out_ref[...] = lse_parts(jnp.stack([first_ref[...], mine]), rate)


def row_third(rate, s_ref, ta_ref, tb_ref, bias_ref, own_ref, out_ref, rows_ref, buf0, buf1, buf2, buf3):
    products(s_ref, ta_ref, (buf0, buf1))
    products(s_ref, tb_ref, (buf2, buf3))
    base = ta_ref.shape[0]
    near = jnp.concatenate(lse_of(buf0, bias_ref, rate) + lse_of(buf1, bias_ref, rate), axis=0)
    far = jnp.concatenate(lse_of(buf2, bias_ref, rate, base) + lse_of(buf3, bias_ref, rate, base), axis=0)
    pair = lse_parts(jnp.stack([near, far]), rate)
    own = own_ref[...]
    low = lax.rem(lax.axis_index("y"), 2) == 0
    rows = jnp.concatenate([jnp.where(low, own, pair), jnp.where(low, pair, own)], axis=0)
    rows_ref[...] = rows
    out_ref[...] = jnp.broadcast_to(rows[None], out_ref.shape)


def row_order(scratch):
    half = scratch.shape[0] // 2
    own = lax.rem(lax.axis_index("y"), 2)

    def row(n):
        at = jnp.where(own == n // half, 0, half)
        return scratch[pl.ds(at + n % half, 1), :]

    return row


def fill_strip(t_ref, sources):
    def fill(n, buf):
        strip = t_ref[pl.ds(pl.multiple_of(n * STRIP, STRIP), STRIP), :]
        at = 0
        for s_ref in sources:
            buf[at : at + s_ref.shape[0], :] = contract(s_ref[...], strip)
            at += s_ref.shape[0]

    return fill


def swap_halves(even, odd):
    low = lax.broadcasted_iota(jnp.int32, even.shape, 1) < LANES // 2
    turn = functools.partial(pltpu.roll, shift=LANES // 2, axis=1)
    return jnp.where(low, even, turn(odd)), jnp.where(low, turn(even), odd)


def fold(value, op):
    out = value[:STEP]
    for r in range(STEP, value.shape[0], STEP):
        out = op(out, value[r : r + STEP])
    return out


def over_strip(sources, bias, strip, each, op):
    got = [None] * (STRIP // LANES)
    at = 0
    for s_ref in sources:
        for r in range(0, s_ref.shape[0], STRIP):
            product = contract(s_ref[r : r + STRIP, :], strip)
            for h, lanes in halves():
                value = fold(each(h, product[:, lanes] + bias[at : at + STRIP, :]), op)
                got[h] = value if got[h] is None else op(got[h], value)
            at += STRIP
    return got


def strips_of(*targets):
    strip = 0
    for t_ref in targets:
        for r in range(0, t_ref.shape[0], STRIP):
            yield strip, t_ref[r : r + STRIP, :]
            strip += 1


def early_kernel(rate, scale, offset, rows_ref, sw_ref, s0, s1, ta_ref, tb_ref, top_ref, ready_ref, bias, ahead):
    high = lax.axis_index("y") // 2
    rows = [sw_ref[pl.ds(2 * z + high, 1), :] for z in range(NZ)]
    weight = jnp.concatenate(swap_halves(jnp.concatenate(rows[0::2], axis=0), jnp.concatenate(rows[1::2], axis=0)), axis=0)
    ready = (jnp.log(weight) + offset) * (1.0 / scale)
    ready_ref[...] = ready
    ahead[...] = ready - rows_ref[...]
    spread_rows(row_order(ahead), bias.shape[0] // LANES, bias)
    for n, strip in strips_of(ta_ref, tb_ref):
        tops = over_strip((s0, s1), bias, strip, lambda h, value: value, jnp.maximum)
        for h, top in enumerate(tops):
            top_ref[2 * n + h : 2 * n + h + 1, :] = jnp.max(top, axis=0, keepdims=True)


def col_kernel(rate, got_ref, rows_ref, ready_ref, top_ref, s0, s1, ta_ref, tb_ref, out_ref, buf0, buf1, bias, ahead, cols, worst):
    lse = lse_parts(got_ref[...], rate)
    potential = ready_ref[...] - lse
    least = jnp.min(lse - rows_ref[...])
    ahead[...] = potential
    spread_rows(row_order(ahead), bias.shape[0] // LANES, bias)
    count = ta_ref.shape[0] // STRIP
    x, c, y = lax.axis_index("x"), lax.axis_index("c"), lax.axis_index("y")
    mine = jnp.where(y >= 2, 1, 0)

    def put(strip, values):
        core = lax.rem(c + strip // count, NC)
        at = lax.rem(strip, count)
        block = lax.rem(x - shift_of(at // 2) + NX, NX) * NC + core
        side = jnp.where(lax.rem(at, 2) == 0, mine, 1 - mine)
        for h, value in enumerate(values):
            cols[side, pl.ds(block * 2 + h, 1), :] = value

    low = None
    for n, strip in strips_of(ta_ref, tb_ref):
        tops = [top_ref[2 * n + h : 2 * n + h + 1, :] - least for h in range(STRIP // LANES)]
        parts = over_strip((s0, s1), bias, strip, lambda h, value: jnp.exp2((value - tops[h]) * rate), jnp.add)
        totals = [jnp.sum(part, axis=0, keepdims=True) for part in parts]
        for total in totals:
            low = total if low is None else jnp.minimum(low, total)
        put(jnp.int32(n), [top + jnp.log2(total) / rate for top, total in zip(tops, totals)])
    worst[...] = low

    @pl.when(jnp.logical_not(jnp.min(worst[...]) >= SAFE))
    def _():
        for other, t_ref in enumerate((ta_ref, tb_ref)):

            def finish(n, buf, other=other):
                put(other * count + n, lse_of(buf, bias, rate))

            all_strips(count, fill_strip(t_ref, (s0, s1)), finish, buf0, buf1)

    for n in range(out_ref.shape[0]):
        out_ref[n, : cols.shape[1], :] = cols[n % 2]
        out_ref[n, cols.shape[1] :, :] = potential


def last_kernel(rate, scale, offset, got_ref, tw_ref, sp_ref, out_ref):
    n_cols = tw_ref.shape[0]
    out_ref[...] = jnp.log(tw_ref[...]) - (lse_parts(got_ref[:, :n_cols, :], rate) * scale - offset)
    place = 2 * (lax.axis_index("x") * NC + lax.axis_index("c"))
    for n in range(2):
        rows = got_ref[place + n, n_cols:, :] * scale
        half = rows.shape[0] // 2
        for odd, part in enumerate(swap_halves(rows[:half], rows[half:])):
            for j in range(half):
                at = 4 * j + 2 * odd + n
                sp_ref[at : at + 1, :] = part[j : j + 1, :]


def cost(mib, flops=0):
    return pl.CostEstimate(flops=int(flops), bytes_accessed=int(mib * MIB), transcendentals=0)


def per_device(source_points, target_points, source_weight, target_weight, target_potential):
    width = source_points.shape[1]
    scale = 1.0 / (EPSILON * math.sqrt(width))
    rate = scale * math.log2(math.e)
    n_rows, n_cols = source_weight.shape[0], target_weight.shape[0]
    rows_all, cols_all = n_rows * NX * NC, n_cols * NZ * NY
    half_rows = n_rows // 2

    def around(n, k):
        return [(i, (i + k) % n) for i in range(n)]

    beside = [(i, i ^ 1) for i in range(NY)]
    across = [(i, i ^ 3) for i in range(NY)]
    z_beside = [[z * NY + y for z in range(NZ) for y in p] for p in ((0, 1), (2, 3))]
    xc_across = [[n * NY + y for n in range(NX * NC) for y in p] for p in ((0, 3), (1, 2))]

    potential = target_potential.reshape(-1, LANES)
    copies = jnp.broadcast_to(source_points[None], (NZ,) + source_points.shape)
    pair_points = lax.ppermute(target_points, "y", across)
    pair_potential = lax.ppermute(potential, "y", across)
    own_potential = lax.ppermute(potential, "c", around(NC, 1))
    mine = jnp.concatenate([target_points, pair_points], axis=0)
    opposite = lax.ppermute(target_points, "x", around(NX, SHIFTS[-1]))
    pieces = [mine] + [lax.ppermute(mine, "x", around(NX, k)) for k in SHIFTS[1:-1]]
    pieces += [opposite, lax.ppermute(opposite, "y", across)]
    own = lax.all_to_all(copies, "z", 0, 0).reshape(-1, width)
    block = NX * mine.shape[0]
    near, bias = pl.pallas_call(
        functools.partial(join_kernel, scale),
        out_shape=[jax.ShapeDtypeStruct((block, width), jnp.bfloat16), jax.ShapeDtypeStruct((2 * block, LANES), f32)],
        in_specs=[pl.BlockSpec(memory_space=pl.ANY)] + [VMEM] * (2 + len(pieces)),
        out_specs=[VMEM] * 2,
        compiler_params=params(16),
        cost_estimate=cost(8),
    )(own, own_potential, pair_potential, *pieces)
    far = lax.ppermute(near, "c", around(NC, 1))
    pair = lax.ppermute(own, "y", beside)
    chunk = own.shape[0]
    sub = half_rows // LANES

    buf = pltpu.VMEM((block, STRIP), f32)
    part = jax.ShapeDtypeStruct((chunk // LANES, LANES), f32)
    first = pl.pallas_call(
        functools.partial(row_first, rate),
        out_shape=part,
        in_specs=[VMEM] * 3,
        out_specs=VMEM,
        scratch_shapes=[buf] * 2,
        compiler_params=params(16),
        cost_estimate=cost(1, 3e10),
    )(own, near, bias)
    second = pl.pallas_call(
        functools.partial(row_second, rate),
        out_shape=part,
        in_specs=[VMEM] * 4,
        out_specs=VMEM,
        scratch_shapes=[buf] * 2,
        compiler_params=params(16),
        cost_estimate=cost(0.25),
    )(own, far, bias, first)
    sent, rows = pl.pallas_call(
        functools.partial(row_third, rate),
        out_shape=[jax.ShapeDtypeStruct((2 * NZ, sub, LANES), f32), jax.ShapeDtypeStruct((sub, LANES), f32)],
        in_specs=[VMEM] * 5,
        out_specs=[VMEM] * 2,
        scratch_shapes=[buf] * 4,
        compiler_params=params(16),
        cost_estimate=cost(16),
    )(pair, near, far, bias, second)
    got = lax.all_to_all(sent, ("z", "y"), 0, 0, axis_index_groups=z_beside)

    strips = 2 * block // STRIP
    held = [pltpu.VMEM((half_rows, LANES), f32), pltpu.VMEM((sub, LANES), f32)]
    tops, ready = pl.pallas_call(
        functools.partial(early_kernel, rate, scale, math.log(cols_all)),
        out_shape=[jax.ShapeDtypeStruct((2 * strips, LANES), f32), jax.ShapeDtypeStruct((sub, LANES), f32)],
        in_specs=[VMEM] * 6,
        out_specs=[VMEM] * 2,
        scratch_shapes=held,
        compiler_params=params(16),
        cost_estimate=cost(16),
    )(rows, source_weight.reshape(-1, LANES), own, pair, near, far)
    sent = pl.pallas_call(
        functools.partial(col_kernel, rate),
        out_shape=jax.ShapeDtypeStruct((2 * NX * NC, n_cols // LANES + sub, LANES), f32),
        in_specs=[VMEM] * 8,
        out_specs=VMEM,
        scratch_shapes=[pltpu.VMEM((half_rows, STRIP), f32)] * 2 + held + [pltpu.VMEM((2, n_cols // LANES, LANES), f32), pltpu.VMEM((1, LANES), f32)],
        compiler_params=params(16),
        cost_estimate=cost(16),
    )(got, rows, ready, tops, own, pair, near, far)
    got = lax.all_to_all(sent, ("x", "c", "y"), 0, 0, axis_index_groups=xc_across)
    potential, updated = pl.pallas_call(
        functools.partial(last_kernel, rate, scale, math.log(rows_all)),
        out_shape=[jax.ShapeDtypeStruct((n // LANES, LANES), f32) for n in (n_rows, n_cols)],
        in_specs=[VMEM] * 2,
        out_specs=[VMEM] * 2,
        compiler_params=params(16),
    )(got, target_weight.reshape(-1, LANES))
    return potential.reshape(-1), updated.reshape(-1)


def solution(mesh):
    grid = Mesh(mesh.devices.reshape(NX, NC, NZ, NY), ("x", "c", "z", "y"))
    return jax.shard_map(
        per_device,
        mesh=grid,
        in_specs=(P(("x", "c", "z", "y"), None), P(("z", "y", "x", "c"), None), P(("x", "c")), P(("z", "y")), P(("z", "y"))),
        out_specs=(P(("x", "c")), P(("z", "y"))),
        check_vma=False,
    )
```

```python
import functools
import math

import jax
import jax.numpy as jnp
from jax import lax
from jax.experimental import pallas as pl
from jax.experimental.pallas import tpu as pltpu
from jax.sharding import Mesh
from jax.sharding import PartitionSpec as P

EPSILON = 0.25
LANES = 128
STRIP = 256
STEP = 64
NX, NC, NZ, NY = 4, 2, 8, 4
SHIFTS = (0, 1, 3, 2)
SAFE = 2.0**-90
VMEM = pl.BlockSpec(memory_space=pltpu.VMEM)
MIB = 1024 * 1024
f32 = jnp.float32


def params(mib):
    return pltpu.CompilerParams(vmem_limit_bytes=mib * MIB)


def contract(a, b):
    return lax.dot_general(a, b, (((1,), (1,)), ((), ())), preferred_element_type=f32)


def spread(row):
    return jnp.broadcast_to(row, (LANES, LANES)).T


def spread_rows(rows_of, count, out):
    for n in range(count):
        out[n * LANES : (n + 1) * LANES, :] = spread(rows_of(n))


def halves():
    return [(h, slice(h * LANES, (h + 1) * LANES)) for h in range(STRIP // LANES)]


def add_and_top(buf, bias, base, lanes):
    top = None
    for r in range(0, buf.shape[0], STEP):
        value = buf[r : r + STEP, lanes] + bias[base + r : base + r + STEP, :]
        buf[r : r + STEP, lanes] = value
        top = value if top is None else jnp.maximum(top, value)
    return jnp.max(top, axis=0, keepdims=True)


def sum_exp(buf, top, lanes, rate):
    total = None
    for r in range(0, buf.shape[0], STEP):
        value = jnp.exp2((buf[r : r + STEP, lanes] - top) * rate)
        total = value if total is None else total + value
    return jnp.sum(total, axis=0, keepdims=True)


def lse_of(buf, bias, rate, base=0):
    out = []
    for _, lanes in halves():
        top = add_and_top(buf, bias, base, lanes)
        out.append(top + jnp.log2(sum_exp(buf, top, lanes, rate)) / rate)
    return out


def lse_parts(parts, rate):
    top = jnp.max(parts, axis=0)
    total = jnp.sum(jnp.exp2((parts - top[None]) * rate), axis=0)
    return top + jnp.log2(total) / rate


def all_strips(count, fill, finish, buf0, buf1):
    fill(0, buf0)

    def pair(p, _):
        fill(2 * p + 1, buf1)
        finish(2 * p, buf0)
        fill(jnp.minimum(2 * p + 2, count - 2), buf0)
        finish(2 * p + 1, buf1)
        return 0

    lax.fori_loop(0, count // 2, pair, 0)


def shift_of(n):
    return jnp.where(n == 2, 3, jnp.where(n == 3, 2, n))


def pack_kernel(targets_ref, tp_ref, packed_ref, own_ref):
    rows = targets_ref.shape[0]
    packed_ref[:rows, :] = targets_ref[...]
    own_ref[...] = tp_ref[...]
    blocks = tp_ref.shape[0] // 2
    rest = jnp.concatenate([tp_ref[pl.ds(half, blocks, stride=2), :] for half in range(2)], axis=1)
    parts = []
    for _ in range(3):
        parts.append(rest.astype(jnp.bfloat16).astype(f32))
        rest = rest - parts[-1]
    parts.append(jnp.zeros_like(rest))
    packed_ref[rows:, :] = jnp.concatenate(parts, axis=0).astype(jnp.bfloat16)


def join_kernel(scale, gate_ref, own_ref, pair_ref, *refs):
    del gate_ref
    *pieces, near_ref, bias_ref, sums_ref = refs
    at = 0
    for piece in pieces:
        near_ref[at : at + piece.shape[0], :] = piece[...]
        at += piece.shape[0]
    near_ref[at:, :] = pair_ref[: near_ref.shape[0] - at, :]
    blocks = sums_ref.shape[0] // 2
    parts = pair_ref[pair_ref.shape[0] - 4 * blocks :, :].astype(f32)
    sums = parts[:blocks] + (parts[blocks : 2 * blocks] + parts[2 * blocks : 3 * blocks])
    for half, lanes in halves():
        sums_ref[half * blocks : (half + 1) * blocks, :] = sums[:, lanes]
    x, c = lax.axis_index("x"), lax.axis_index("c")
    row = 0
    for other in range(NC):
        for k in SHIFTS:
            block = lax.rem(x - k + NX, NX) * NC + lax.rem(c + other, NC)
            values = [own_ref[pl.ds(block * 2 + half, 1), :] for half in range(2)]
            values += [sums_ref[pl.ds(half * blocks + block, 1), :] for half in range(2)]
            for value in values:
                bias_ref[row * LANES : (row + 1) * LANES, :] = spread(value * (1.0 / scale))
                row += 1


def row_part(rate, s_ref, t_ref, bias_ref, base, bufs):
    for n, buf in enumerate(bufs):
        buf[...] = contract(t_ref[...], s_ref[n * STRIP : (n + 1) * STRIP, :])
    return jnp.concatenate([row for buf in bufs for row in lse_of(buf, bias_ref, rate, base)], axis=0)


def row_near(rate, s_ref, t_ref, bias_ref, out_ref, buf0, buf1):
    out_ref[...] = row_part(rate, s_ref, t_ref, bias_ref, 0, (buf0, buf1))


def row_far(rate, own_ref, pair_ref, t_ref, bias_ref, own_near, pair_near, out_ref, rows_ref, buf0, buf1, buf2, buf3):
    base = t_ref.shape[0]
    own = lse_parts(jnp.stack([own_near[...], row_part(rate, own_ref, t_ref, bias_ref, base, (buf0, buf1))]), rate)
    pair = lse_parts(jnp.stack([pair_near[...], row_part(rate, pair_ref, t_ref, bias_ref, base, (buf2, buf3))]), rate)
    low = lax.rem(lax.axis_index("y"), 2) == 0
    rows = jnp.concatenate([jnp.where(low, own, pair), jnp.where(low, pair, own)], axis=0)
    rows_ref[...] = rows
    out_ref[...] = jnp.broadcast_to(rows[None], out_ref.shape)


def row_order(scratch):
    half = scratch.shape[0] // 2
    own = lax.rem(lax.axis_index("y"), 2)

    def row(n):
        at = jnp.where(own == n // half, 0, half)
        return scratch[pl.ds(at + n % half, 1), :]

    return row


def fill_strip(t_ref, sources):
    def fill(n, buf):
        strip = t_ref[pl.ds(pl.multiple_of(n * STRIP, STRIP), STRIP), :]
        at = 0
        for s_ref in sources:
            buf[at : at + s_ref.shape[0], :] = contract(s_ref[...], strip)
            at += s_ref.shape[0]

    return fill


def swap_halves(even, odd):
    low = lax.broadcasted_iota(jnp.int32, even.shape, 1) < LANES // 2
    turn = functools.partial(pltpu.roll, shift=LANES // 2, axis=1)
    return jnp.where(low, even, turn(odd)), jnp.where(low, turn(even), odd)


def fold(value, op):
    out = value[:STEP]
    for r in range(STEP, value.shape[0], STEP):
        out = op(out, value[r : r + STEP])
    return out


def over_strip(sources, bias, strip, each, op):
    got = [None] * (STRIP // LANES)
    at = 0
    for s_ref in sources:
        for r in range(0, s_ref.shape[0], STRIP):
            product = contract(s_ref[r : r + STRIP, :], strip)
            for h, lanes in halves():
                value = fold(each(h, product[:, lanes] + bias[at : at + STRIP, :]), op)
                got[h] = value if got[h] is None else op(got[h], value)
            at += STRIP
    return got


def strips_of(*targets):
    strip = 0
    for t_ref in targets:
        for r in range(0, t_ref.shape[0], STRIP):
            yield strip, t_ref[r : r + STRIP, :]
            strip += 1


def early_kernel(rate, scale, offset, rows_ref, sw_ref, s0, s1, ta_ref, tb_ref, top_ref, ready_ref, bias, ahead):
    high = lax.axis_index("y") // 2
    rows = [sw_ref[pl.ds(2 * z + high, 1), :] for z in range(NZ)]
    weight = jnp.concatenate(swap_halves(jnp.concatenate(rows[0::2], axis=0), jnp.concatenate(rows[1::2], axis=0)), axis=0)
    ready = (jnp.log(weight) + offset) * (1.0 / scale)
    ready_ref[...] = ready
    ahead[...] = ready - rows_ref[...]
    spread_rows(row_order(ahead), bias.shape[0] // LANES, bias)
    for n, strip in strips_of(ta_ref, tb_ref):
        tops = over_strip((s0, s1), bias, strip, lambda h, value: value, jnp.maximum)
        for h, top in enumerate(tops):
            top_ref[2 * n + h : 2 * n + h + 1, :] = jnp.max(top, axis=0, keepdims=True)


def col_kernel(rate, got_ref, rows_ref, ready_ref, top_ref, s0, s1, ta_ref, tb_ref, out_ref, buf0, buf1, bias, ahead, cols, worst):
    lse = lse_parts(got_ref[...], rate)
    potential = ready_ref[...] - lse
    least = jnp.min(lse - rows_ref[...])
    ahead[...] = potential
    spread_rows(row_order(ahead), bias.shape[0] // LANES, bias)
    count = ta_ref.shape[0] // STRIP
    x, c, y = lax.axis_index("x"), lax.axis_index("c"), lax.axis_index("y")
    mine = jnp.where(y >= 2, 1, 0)

    def put(strip, values):
        core = lax.rem(c + strip // count, NC)
        at = lax.rem(strip, count)
        block = lax.rem(x - shift_of(at // 2) + NX, NX) * NC + core
        side = jnp.where(lax.rem(at, 2) == 0, mine, 1 - mine)
        for h, value in enumerate(values):
            cols[side, pl.ds(block * 2 + h, 1), :] = value

    low = None
    for n, strip in strips_of(ta_ref, tb_ref):
        tops = [top_ref[2 * n + h : 2 * n + h + 1, :] - least for h in range(STRIP // LANES)]
        parts = over_strip((s0, s1), bias, strip, lambda h, value: jnp.exp2((value - tops[h]) * rate), jnp.add)
        totals = [jnp.sum(part, axis=0, keepdims=True) for part in parts]
        for total in totals:
            low = total if low is None else jnp.minimum(low, total)
        put(jnp.int32(n), [top + jnp.log2(total) / rate for top, total in zip(tops, totals)])
    worst[...] = low

    @pl.when(jnp.logical_not(jnp.min(worst[...]) >= SAFE))
    def _():
        for other, t_ref in enumerate((ta_ref, tb_ref)):

            def finish(n, buf, other=other):
                put(other * count + n, lse_of(buf, bias, rate))

            all_strips(count, fill_strip(t_ref, (s0, s1)), finish, buf0, buf1)

    for n in range(out_ref.shape[0]):
        out_ref[n, : cols.shape[1], :] = cols[n % 2]
        out_ref[n, cols.shape[1] :, :] = potential


def last_kernel(rate, scale, offset, got_ref, tw_ref, sp_ref, out_ref):
    n_cols = tw_ref.shape[0]
    out_ref[...] = jnp.log(tw_ref[...]) - (lse_parts(got_ref[:, :n_cols, :], rate) * scale - offset)
    place = 2 * (lax.axis_index("x") * NC + lax.axis_index("c"))
    for n in range(2):
        rows = got_ref[place + n, n_cols:, :] * scale
        half = rows.shape[0] // 2
        for odd, part in enumerate(swap_halves(rows[:half], rows[half:])):
            for j in range(half):
                at = 4 * j + 2 * odd + n
                sp_ref[at : at + 1, :] = part[j : j + 1, :]


def cost(mib, flops=0):
    return pl.CostEstimate(flops=int(flops), bytes_accessed=int(mib * MIB), transcendentals=0)


def per_device(source_points, target_points, source_weight, target_weight, target_potential):
    width = source_points.shape[1]
    scale = 1.0 / (EPSILON * math.sqrt(width))
    rate = scale * math.log2(math.e)
    n_rows, n_cols = source_weight.shape[0], target_weight.shape[0]
    rows_all, cols_all = n_rows * NX * NC, n_cols * NZ * NY
    half_rows = n_rows // 2

    def around(n, k):
        return [(i, (i + k) % n) for i in range(n)]

    beside = [(i, i ^ 1) for i in range(NY)]
    across = [(i, i ^ 3) for i in range(NY)]
    z_beside = [[z * NY + y for z in range(NZ) for y in p] for p in ((0, 1), (2, 3))]
    xc_across = [[n * NY + y for n in range(NX * NC) for y in p] for p in ((0, 3), (1, 2))]

    potential = target_potential.reshape(-1, LANES)
    copies = jnp.broadcast_to(source_points[None], (NZ,) + source_points.shape)
    pair_points = lax.ppermute(target_points, "y", across)
    mine = jnp.concatenate([target_points, pair_points], axis=0)
    opposite = lax.ppermute(target_points, "x", around(NX, SHIFTS[-1]))
    pieces = [mine] + [lax.ppermute(mine, "x", around(NX, k)) for k in SHIFTS[1:-1]] + [opposite]
    packed, own_potential = pl.pallas_call(
        pack_kernel,
        out_shape=[
            jax.ShapeDtypeStruct((opposite.shape[0] + 2 * potential.shape[0], width), jnp.bfloat16),
            jax.ShapeDtypeStruct(potential.shape, f32),
        ],
        in_specs=[VMEM] * 2,
        out_specs=[VMEM] * 2,
        compiler_params=params(16),
        cost_estimate=cost(0.001),
    )(opposite, potential)
    pair_packed = lax.ppermute(packed, "y", across)
    own = lax.all_to_all(copies, "z", 0, 0).reshape(-1, width)
    block = NX * mine.shape[0]
    near, bias = pl.pallas_call(
        functools.partial(join_kernel, scale),
        out_shape=[jax.ShapeDtypeStruct((block, width), jnp.bfloat16), jax.ShapeDtypeStruct((2 * block, LANES), f32)],
        in_specs=[pl.BlockSpec(memory_space=pl.ANY)] + [VMEM] * (2 + len(pieces)),
        out_specs=[VMEM] * 2,
        scratch_shapes=[pltpu.VMEM(potential.shape, f32)],
        compiler_params=params(16),
        cost_estimate=cost(8),
    )(own, own_potential, pair_packed, *pieces)
    far = lax.ppermute(near, "c", around(NC, 1))
    pair = lax.ppermute(own, "y", beside)
    chunk = own.shape[0]
    sub = half_rows // LANES

    buf = pltpu.VMEM((block, STRIP), f32)
    part = jax.ShapeDtypeStruct((chunk // LANES, LANES), f32)
    def over_near(sources, weight):
        return pl.pallas_call(
            functools.partial(row_near, rate),
            out_shape=part,
            in_specs=[VMEM] * 3,
            out_specs=VMEM,
            scratch_shapes=[buf] * 2,
            compiler_params=params(16),
            cost_estimate=weight,
        )(sources, near, bias)

    own_near, pair_near = over_near(own, cost(1, 3e10)), over_near(pair, cost(0.25))
    sent, rows = pl.pallas_call(
        functools.partial(row_far, rate),
        out_shape=[jax.ShapeDtypeStruct((2 * NZ, sub, LANES), f32), jax.ShapeDtypeStruct((sub, LANES), f32)],
        in_specs=[VMEM] * 6,
        out_specs=[VMEM] * 2,
        scratch_shapes=[buf] * 4,
        compiler_params=params(16),
        cost_estimate=cost(16),
    )(own, pair, far, bias, own_near, pair_near)
    got = lax.all_to_all(sent, ("z", "y"), 0, 0, axis_index_groups=z_beside)

    strips = 2 * block // STRIP
    held = [pltpu.VMEM((half_rows, LANES), f32), pltpu.VMEM((sub, LANES), f32)]
    tops, ready = pl.pallas_call(
        functools.partial(early_kernel, rate, scale, math.log(cols_all)),
        out_shape=[jax.ShapeDtypeStruct((2 * strips, LANES), f32), jax.ShapeDtypeStruct((sub, LANES), f32)],
        in_specs=[VMEM] * 6,
        out_specs=[VMEM] * 2,
        scratch_shapes=held,
        compiler_params=params(16),
        cost_estimate=cost(16),
    )(rows, source_weight.reshape(-1, LANES), own, pair, near, far)
    sent = pl.pallas_call(
        functools.partial(col_kernel, rate),
        out_shape=jax.ShapeDtypeStruct((2 * NX * NC, n_cols // LANES + sub, LANES), f32),
        in_specs=[VMEM] * 8,
        out_specs=VMEM,
        scratch_shapes=[pltpu.VMEM((half_rows, STRIP), f32)] * 2 + held + [pltpu.VMEM((2, n_cols // LANES, LANES), f32), pltpu.VMEM((1, LANES), f32)],
        compiler_params=params(16),
        cost_estimate=cost(16),
    )(got, rows, ready, tops, own, pair, near, far)
    got = lax.all_to_all(sent, ("x", "c", "y"), 0, 0, axis_index_groups=xc_across)
    potential, updated = pl.pallas_call(
        functools.partial(last_kernel, rate, scale, math.log(rows_all)),
        out_shape=[jax.ShapeDtypeStruct((n // LANES, LANES), f32) for n in (n_rows, n_cols)],
        in_specs=[VMEM] * 2,
        out_specs=[VMEM] * 2,
        compiler_params=params(16),
    )(got, target_weight.reshape(-1, LANES))
    return potential.reshape(-1), updated.reshape(-1)


def solution(mesh):
    grid = Mesh(mesh.devices.reshape(NX, NC, NZ, NY), ("x", "c", "z", "y"))
    return jax.shard_map(
        per_device,
        mesh=grid,
        in_specs=(P(("x", "c", "z", "y"), None), P(("z", "y", "x", "c"), None), P(("x", "c")), P(("z", "y")), P(("z", "y"))),
        out_specs=(P(("x", "c")), P(("z", "y"))),
        check_vma=False,
    )
```

```python
import functools
import math

import jax
import jax.numpy as jnp
from jax import lax
from jax.experimental import pallas as pl
from jax.experimental.pallas import tpu as pltpu
from jax.sharding import Mesh
from jax.sharding import PartitionSpec as P

EPSILON = 0.25
LANES = 128
STRIP = 256
STEP = 64
NX, NC, NZ, NY = 4, 2, 8, 4
SHIFTS = (0, 1, 3, 2)
SAFE = 2.0**-90
VMEM = pl.BlockSpec(memory_space=pltpu.VMEM)
MIB = 1024 * 1024
f32 = jnp.float32


def params(mib):
    return pltpu.CompilerParams(vmem_limit_bytes=mib * MIB)


def contract(a, b):
    return lax.dot_general(a, b, (((1,), (1,)), ((), ())), preferred_element_type=f32)


def spread(row):
    return jnp.broadcast_to(row, (LANES, LANES)).T


def spread_rows(rows_of, count, out):
    for n in range(count):
        out[n * LANES : (n + 1) * LANES, :] = spread(rows_of(n))


def halves():
    return [(h, slice(h * LANES, (h + 1) * LANES)) for h in range(STRIP // LANES)]


def add_and_top(buf, bias, base, lanes):
    top = None
    for r in range(0, buf.shape[0], STEP):
        value = buf[r : r + STEP, lanes] + bias[base + r : base + r + STEP, :]
        buf[r : r + STEP, lanes] = value
        top = value if top is None else jnp.maximum(top, value)
    return jnp.max(top, axis=0, keepdims=True)


def sum_exp(buf, top, lanes, rate):
    total = None
    for r in range(0, buf.shape[0], STEP):
        value = jnp.exp2((buf[r : r + STEP, lanes] - top) * rate)
        total = value if total is None else total + value
    return jnp.sum(total, axis=0, keepdims=True)


def lse_of(buf, bias, rate, base=0):
    out = []
    for _, lanes in halves():
        top = add_and_top(buf, bias, base, lanes)
        out.append(top + jnp.log2(sum_exp(buf, top, lanes, rate)) / rate)
    return out


def lse_parts(parts, rate):
    top = jnp.max(parts, axis=0)
    total = jnp.sum(jnp.exp2((parts - top[None]) * rate), axis=0)
    return top + jnp.log2(total) / rate


def all_strips(count, fill, finish, buf0, buf1):
    fill(0, buf0)

    def pair(p, _):
        fill(2 * p + 1, buf1)
        finish(2 * p, buf0)
        fill(jnp.minimum(2 * p + 2, count - 2), buf0)
        finish(2 * p + 1, buf1)
        return 0

    lax.fori_loop(0, count // 2, pair, 0)


def shift_of(n):
    return jnp.where(n == 2, 3, jnp.where(n == 3, 2, n))


def pack_kernel(targets_ref, tp_ref, packed_ref, own_ref):
    rows = targets_ref.shape[0]
    packed_ref[:rows, :] = targets_ref[...]
    own_ref[...] = tp_ref[...]
    blocks = tp_ref.shape[0] // 2
    rest = jnp.concatenate([tp_ref[pl.ds(half, blocks, stride=2), :] for half in range(2)], axis=1)
    parts = []
    for _ in range(3):
        parts.append(rest.astype(jnp.bfloat16).astype(f32))
        rest = rest - parts[-1]
    parts.append(jnp.zeros_like(rest))
    packed_ref[rows:, :] = jnp.concatenate(parts, axis=0).astype(jnp.bfloat16)


def join_kernel(scale, gate_ref, own_ref, pair_ref, *refs):
    del gate_ref
    *pieces, near_ref, bias_ref, sums_ref = refs
    at = 0
    for piece in pieces:
        near_ref[at : at + piece.shape[0], :] = piece[...]
        at += piece.shape[0]
    near_ref[at:, :] = pair_ref[: near_ref.shape[0] - at, :]
    blocks = sums_ref.shape[0] // 2
    parts = pair_ref[pair_ref.shape[0] - 4 * blocks :, :].astype(f32)
    sums = parts[:blocks] + (parts[blocks : 2 * blocks] + parts[2 * blocks : 3 * blocks])
    for half, lanes in halves():
        sums_ref[half * blocks : (half + 1) * blocks, :] = sums[:, lanes]
    x, c = lax.axis_index("x"), lax.axis_index("c")
    row = 0
    for other in range(NC):
        for k in SHIFTS:
            block = lax.rem(x - k + NX, NX) * NC + lax.rem(c + other, NC)
            values = [own_ref[pl.ds(block * 2 + half, 1), :] for half in range(2)]
            values += [sums_ref[pl.ds(half * blocks + block, 1), :] for half in range(2)]
            for value in values:
                bias_ref[row * LANES : (row + 1) * LANES, :] = spread(value * (1.0 / scale))
                row += 1


def row_part(rate, s_ref, t_ref, bias_ref, base, bufs):
    for n, buf in enumerate(bufs):
        buf[...] = contract(t_ref[...], s_ref[n * STRIP : (n + 1) * STRIP, :])
    return jnp.concatenate([row for buf in bufs for row in lse_of(buf, bias_ref, rate, base)], axis=0)


def row_near(rate, s_ref, t_ref, bias_ref, out_ref, buf0, buf1):
    out_ref[...] = row_part(rate, s_ref, t_ref, bias_ref, 0, (buf0, buf1))


def row_far(rate, own_ref, pair_ref, t_ref, bias_ref, own_near, pair_near, out_ref, rows_ref, buf0, buf1, buf2, buf3):
    base = t_ref.shape[0]
    own = lse_parts(jnp.stack([own_near[...], row_part(rate, own_ref, t_ref, bias_ref, base, (buf0, buf1))]), rate)
    pair = lse_parts(jnp.stack([pair_near[...], row_part(rate, pair_ref, t_ref, bias_ref, base, (buf2, buf3))]), rate)
    low = lax.rem(lax.axis_index("y"), 2) == 0
    rows = jnp.concatenate([jnp.where(low, own, pair), jnp.where(low, pair, own)], axis=0)
    rows_ref[...] = rows
    out_ref[...] = jnp.broadcast_to(rows[None], out_ref.shape)


def row_order(scratch):
    half = scratch.shape[0] // 2
    own = lax.rem(lax.axis_index("y"), 2)

    def row(n):
        at = jnp.where(own == n // half, 0, half)
        return scratch[pl.ds(at + n % half, 1), :]

    return row


def fill_strip(t_ref, sources):
    def fill(n, buf):
        strip = t_ref[pl.ds(pl.multiple_of(n * STRIP, STRIP), STRIP), :]
        at = 0
        for s_ref in sources:
            buf[at : at + s_ref.shape[0], :] = contract(s_ref[...], strip)
            at += s_ref.shape[0]

    return fill


def swap_halves(even, odd):
    low = lax.broadcasted_iota(jnp.int32, even.shape, 1) < LANES // 2
    turn = functools.partial(pltpu.roll, shift=LANES // 2, axis=1)
    return jnp.where(low, even, turn(odd)), jnp.where(low, turn(even), odd)


def fold(value, op):
    out = value[:STEP]
    for r in range(STEP, value.shape[0], STEP):
        out = op(out, value[r : r + STEP])
    return out


def over_strip(sources, bias, strip, each, op):
    got = [None] * (STRIP // LANES)
    at = 0
    for s_ref in sources:
        for r in range(0, s_ref.shape[0], STRIP):
            product = contract(s_ref[r : r + STRIP, :], strip)
            for h, lanes in halves():
                value = fold(each(h, product[:, lanes] + bias[at : at + STRIP, :]), op)
                got[h] = value if got[h] is None else op(got[h], value)
            at += STRIP
    return got


def strips_of(*targets):
    strip = 0
    for t_ref in targets:
        for r in range(0, t_ref.shape[0], STRIP):
            yield strip, t_ref[r : r + STRIP, :]
            strip += 1


def early_kernel(rate, scale, offset, rows_ref, sw_ref, s0, s1, ta_ref, tb_ref, top_ref, ready_ref, bias, ahead):
    high = lax.axis_index("y") // 2
    rows = [sw_ref[pl.ds(2 * z + high, 1), :] for z in range(NZ)]
    weight = jnp.concatenate(swap_halves(jnp.concatenate(rows[0::2], axis=0), jnp.concatenate(rows[1::2], axis=0)), axis=0)
    ready = (jnp.log(weight) + offset) * (1.0 / scale)
    ready_ref[...] = ready
    ahead[...] = ready - rows_ref[...]
    spread_rows(row_order(ahead), bias.shape[0] // LANES, bias)
    for n, strip in strips_of(ta_ref, tb_ref):
        tops = over_strip((s0, s1), bias, strip, lambda h, value: value, jnp.maximum)
        for h, top in enumerate(tops):
            top_ref[2 * n + h : 2 * n + h + 1, :] = jnp.max(top, axis=0, keepdims=True)


def col_kernel(rate, got_ref, rows_ref, ready_ref, top_ref, s0, s1, ta_ref, tb_ref, out_ref, buf0, buf1, bias, ahead, cols, worst):
    lse = lse_parts(got_ref[...], rate)
    potential = ready_ref[...] - lse
    least = jnp.min(lse - rows_ref[...])
    ahead[...] = potential
    spread_rows(row_order(ahead), bias.shape[0] // LANES, bias)
    count = ta_ref.shape[0] // STRIP
    x, c, y = lax.axis_index("x"), lax.axis_index("c"), lax.axis_index("y")
    mine = jnp.where(y >= 2, 1, 0)

    def put(strip, values):
        core = lax.rem(c + strip // count, NC)
        at = lax.rem(strip, count)
        block = lax.rem(x - shift_of(at // 2) + NX, NX) * NC + core
        side = jnp.where(lax.rem(at, 2) == 0, mine, 1 - mine)
        for h, value in enumerate(values):
            cols[side, pl.ds(block * 2 + h, 1), :] = value

    low = None
    for n, strip in strips_of(ta_ref, tb_ref):
        tops = [top_ref[2 * n + h : 2 * n + h + 1, :] - least for h in range(STRIP // LANES)]
        parts = over_strip((s0, s1), bias, strip, lambda h, value: jnp.exp2((value - tops[h]) * rate), jnp.add)
        totals = [jnp.sum(part, axis=0, keepdims=True) for part in parts]
        for total in totals:
            low = total if low is None else jnp.minimum(low, total)
        put(jnp.int32(n), [top + jnp.log2(total) / rate for top, total in zip(tops, totals)])
    worst[...] = low

    @pl.when(jnp.logical_not(jnp.min(worst[...]) >= SAFE))
    def _():
        for other, t_ref in enumerate((ta_ref, tb_ref)):

            def finish(n, buf, other=other):
                put(other * count + n, lse_of(buf, bias, rate))

            all_strips(count, fill_strip(t_ref, (s0, s1)), finish, buf0, buf1)

    for n in range(out_ref.shape[0]):
        out_ref[n, : cols.shape[1], :] = cols[n % 2]
        out_ref[n, cols.shape[1] :, :] = potential


def last_kernel(rate, scale, offset, got_ref, tw_ref, sp_ref, out_ref):
    n_cols = tw_ref.shape[0]
    out_ref[...] = jnp.log(tw_ref[...]) - (lse_parts(got_ref[:, :n_cols, :], rate) * scale - offset)
    place = 2 * (lax.axis_index("x") * NC + lax.axis_index("c"))
    for n in range(2):
        rows = got_ref[place + n, n_cols:, :] * scale
        half = rows.shape[0] // 2
        for odd, part in enumerate(swap_halves(rows[:half], rows[half:])):
            for j in range(half):
                at = 4 * j + 2 * odd + n
                sp_ref[at : at + 1, :] = part[j : j + 1, :]


def cost(mib, flops=0):
    return pl.CostEstimate(flops=int(flops), bytes_accessed=int(mib * MIB), transcendentals=0)


def per_device(source_points, target_points, source_weight, target_weight, target_potential):
    width = source_points.shape[1]
    scale = 1.0 / (EPSILON * math.sqrt(width))
    rate = scale * math.log2(math.e)
    n_rows, n_cols = source_weight.shape[0], target_weight.shape[0]
    rows_all, cols_all = n_rows * NX * NC, n_cols * NZ * NY
    half_rows = n_rows // 2

    def around(n, k):
        return [(i, (i + k) % n) for i in range(n)]

    beside = [(i, i ^ 1) for i in range(NY)]
    across = [(i, i ^ 3) for i in range(NY)]
    z_beside = [[z * NY + y for z in range(NZ) for y in p] for p in ((0, 1), (2, 3))]
    xc_across = [[n * NY + y for n in range(NX * NC) for y in p] for p in ((0, 3), (1, 2))]

    potential = target_potential.reshape(-1, LANES)
    copies = jnp.broadcast_to(source_points[None], (NZ,) + source_points.shape)
    pair_points = lax.ppermute(target_points, "y", across)
    mine = jnp.concatenate([target_points, pair_points], axis=0)
    opposite = lax.ppermute(target_points, "x", around(NX, SHIFTS[-1]))
    pieces = [mine] + [lax.ppermute(mine, "x", around(NX, k)) for k in SHIFTS[1:-1]] + [opposite]
    near_potential = lax.ppermute(potential, "c", around(NC, 1))
    packed, own_potential = pl.pallas_call(
        pack_kernel,
        out_shape=[
            jax.ShapeDtypeStruct((opposite.shape[0] + 2 * potential.shape[0], width), jnp.bfloat16),
            jax.ShapeDtypeStruct(potential.shape, f32),
        ],
        in_specs=[VMEM] * 2,
        out_specs=[VMEM] * 2,
        compiler_params=params(16),
        cost_estimate=cost(0.001),
    )(opposite, near_potential)
    pair_packed = lax.ppermute(packed, "y", across)
    own = lax.all_to_all(copies, "z", 0, 0).reshape(-1, width)
    block = NX * mine.shape[0]
    near, bias = pl.pallas_call(
        functools.partial(join_kernel, scale),
        out_shape=[jax.ShapeDtypeStruct((block, width), jnp.bfloat16), jax.ShapeDtypeStruct((2 * block, LANES), f32)],
        in_specs=[pl.BlockSpec(memory_space=pl.ANY)] + [VMEM] * (2 + len(pieces)),
        out_specs=[VMEM] * 2,
        scratch_shapes=[pltpu.VMEM(potential.shape, f32)],
        compiler_params=params(16),
        cost_estimate=cost(8),
    )(own, own_potential, pair_packed, *pieces)
    far = lax.ppermute(near, "c", around(NC, 1))
    pair = lax.ppermute(own, "y", beside)
    chunk = own.shape[0]
    sub = half_rows // LANES

    buf = pltpu.VMEM((block, STRIP), f32)
    part = jax.ShapeDtypeStruct((chunk // LANES, LANES), f32)
    def over_near(sources, weight):
        return pl.pallas_call(
            functools.partial(row_near, rate),
            out_shape=part,
            in_specs=[VMEM] * 3,
            out_specs=VMEM,
            scratch_shapes=[buf] * 2,
            compiler_params=params(16),
            cost_estimate=weight,
        )(sources, near, bias)

    own_near, pair_near = over_near(own, cost(1, 3e10)), over_near(pair, cost(0.25))
    sent, rows = pl.pallas_call(
        functools.partial(row_far, rate),
        out_shape=[jax.ShapeDtypeStruct((2 * NZ, sub, LANES), f32), jax.ShapeDtypeStruct((sub, LANES), f32)],
        in_specs=[VMEM] * 6,
        out_specs=[VMEM] * 2,
        scratch_shapes=[buf] * 4,
        compiler_params=params(16),
        cost_estimate=cost(16),
    )(own, pair, far, bias, own_near, pair_near)
    got = lax.all_to_all(sent, ("z", "y"), 0, 0, axis_index_groups=z_beside)

    strips = 2 * block // STRIP
    held = [pltpu.VMEM((half_rows, LANES), f32), pltpu.VMEM((sub, LANES), f32)]
    tops, ready = pl.pallas_call(
        functools.partial(early_kernel, rate, scale, math.log(cols_all)),
        out_shape=[jax.ShapeDtypeStruct((2 * strips, LANES), f32), jax.ShapeDtypeStruct((sub, LANES), f32)],
        in_specs=[VMEM] * 6,
        out_specs=[VMEM] * 2,
        scratch_shapes=held,
        compiler_params=params(16),
        cost_estimate=cost(16),
    )(rows, source_weight.reshape(-1, LANES), own, pair, near, far)
    sent = pl.pallas_call(
        functools.partial(col_kernel, rate),
        out_shape=jax.ShapeDtypeStruct((2 * NX * NC, n_cols // LANES + sub, LANES), f32),
        in_specs=[VMEM] * 8,
        out_specs=VMEM,
        scratch_shapes=[pltpu.VMEM((half_rows, STRIP), f32)] * 2 + held + [pltpu.VMEM((2, n_cols // LANES, LANES), f32), pltpu.VMEM((1, LANES), f32)],
        compiler_params=params(16),
        cost_estimate=cost(16),
    )(got, rows, ready, tops, own, pair, near, far)
    got = lax.all_to_all(sent, ("x", "c", "y"), 0, 0, axis_index_groups=xc_across)
    potential, updated = pl.pallas_call(
        functools.partial(last_kernel, rate, scale, math.log(rows_all)),
        out_shape=[jax.ShapeDtypeStruct((n // LANES, LANES), f32) for n in (n_rows, n_cols)],
        in_specs=[VMEM] * 2,
        out_specs=[VMEM] * 2,
        compiler_params=params(16),
    )(got, target_weight.reshape(-1, LANES))
    return potential.reshape(-1), updated.reshape(-1)


def solution(mesh):
    grid = Mesh(mesh.devices.reshape(NX, NC, NZ, NY), ("x", "c", "z", "y"))
    return jax.shard_map(
        per_device,
        mesh=grid,
        in_specs=(P(("x", "c", "z", "y"), None), P(("z", "y", "x", "c"), None), P(("x", "c")), P(("z", "y")), P(("z", "y"))),
        out_specs=(P(("x", "c")), P(("z", "y"))),
        check_vma=False,
    )
```
